32 devices in a mesh: replica: 2 (over x), node: 8 (over z, y), local: 2 (over core).
Axes of the slice: x: 2, y: 2, z: 4, core: 2. Of those that a mesh axis runs over, the one named last changes fastest.
Arguments:
- gate_pre: bfloat16 [2048, 14336], P(('replica', 'node'), 'local'), may hold values from -6 to 6
- up_pre: bfloat16 [2048, 14336], P(('replica', 'node'), 'local'), may hold values from -6 to 6
- upstream: bfloat16 [2048, 4096], P(('replica', 'node')), may hold values from -6 to 6
- weight_codes: bfloat16 [4096, 14336], P('node', 'local'), may hold values from -0.046875 to 0.046875
- scales: bfloat16 [4096, 112], P('node', 'local'), may hold values from 0.5 to 4
Outputs:
- layer_out: bfloat16 [2048, 4096], P(('replica', 'node', 'local'))
- gate_grad: bfloat16 [2048, 14336], P(('replica', 'node'), 'local')
- up_grad: bfloat16 [2048, 14336], P(('replica', 'node'), 'local')
- weight_grad: bfloat16 [4096, 14336], P(('replica', 'node'), 'local')
The draws below stay inside these ranges and needn't reach their ends.
All inputs are finite; a program needn't handle non-finite values.
Results may differ from the reference program's by a relative error of at most 0.013.
Values may be sent and summed in bfloat16 or wider, within the bound.
No kernel may reach another device: no remote copies, remote signals or barrier semaphores. Data moves between devices by JAX's collectives and lax.ppermute only.
A program may use at most 384 MiB of HBM per device.

```python
import math
import jax
import jax.numpy as jnp
from jax import lax

D = 4096
FF = 14336
BLOCK = 128
TOK_GRP = 128
TOKENS = 2048
N_REPLICA = 2
N_NODE = 8
N_LOCAL = 2


def raised(entries, rng, source, target, shards_of, factor):
    owner, partner = [(jnp.arange(entries.shape[dim]) // (entries.shape[dim] // shards_of)).reshape([-1 if axis == dim else 1 for axis in range(entries.ndim)]) for dim in (source, target)]
    chosen = jax.random.permutation(rng, shards_of)[partner]
    strong = (owner == chosen) | (owner == (partner + shards_of // 2) % shards_of)
    return jnp.where(strong, factor * entries, entries)


def levels(rng, extent, pieces, smallest, top_value):
    def one(position, shards_of):
        draws = jax.random.uniform(jax.random.fold_in(jax.random.fold_in(rng, 6), position), (shards_of,), jnp.float32, smallest / len(pieces), top_value / len(pieces))
        return jnp.repeat(jnp.exp(draws), extent[position] // shards_of).reshape((-1,) + (1,) * (len(extent) - position - 1))

    level = one(*pieces[0])
    for cut in pieces[1:]:
        level = level * one(*cut)
    return level


def noise(rng, shape, width, most, cuts=(), kind=jnp.bfloat16):
    result = jax.random.normal(rng, shape, jnp.float32) * width
    if len(cuts) > 0:
        result = levels(rng, shape, cuts, -0.22, 0.18) * result
    return jnp.clip(result, min=-most, max=most).astype(kind)


def gaussian_with(rng, shape, scale, most, cuts, heavy, kind=jnp.bfloat16):
    drawn = scale * jax.random.normal(rng, shape, jnp.float32)
    if cuts:
        drawn = drawn * levels(rng, shape, cuts, -0.22, 0.18)
    return jnp.clip(raised(drawn, jax.random.fold_in(rng, 3), *heavy), -most, most).astype(kind)


def setup_inputs(seed: int = 0) -> dict:
    key_of = jax.random.split(jax.random.key(seed), 6)
    gate_pre = noise(key_of[0], (TOKENS, FF), 1.0, 6.0, ((0, 16), (1, 2)))
    up_pre = noise(key_of[1], (TOKENS, FF), 1.0, 6.0, ((0, 16), (1, 2)))
    upstream = gaussian_with(key_of[2], (TOKENS, D), 1.0, 6.0, ((0, 16),), (0, 1, 16, 2.0))
    weight_codes = noise(key_of[3], (D, FF), FF ** -0.5, 0.046875, ((0, 8), (1, 2)))
    scales = jnp.clip(jnp.exp(math.log(4.0) - 2.0794415 * jax.random.uniform(key_of[4], (D, FF // BLOCK), jnp.float32) ** levels(key_of[4], (D, FF // BLOCK), ((0, 8), (1, 2)), -0.2, 0.2)), 0.5, 4.0).astype(jnp.bfloat16)
    return {"gate_pre": gate_pre, "up_pre": up_pre, "upstream": upstream, "weight_codes": weight_codes, "scales": scales}


def dequantize(code_rows, scale_rows):
    grouped = code_rows.astype(jnp.float32).reshape(code_rows.shape[0], scale_rows.shape[1], -1)
    scaled = grouped * scale_rows.astype(jnp.float32)[:, :, None]
    return scaled.reshape(code_rows.shape).astype(jnp.bfloat16)


def contract_rows(left, right):
    return lax.dot_general(left, right, (((0,), (0,)), ((), ())), preferred_element_type=jnp.float32)


def contract_cols(left, right):
    return lax.dot_general(left, right, (((1,), (1,)), ((), ())), preferred_element_type=jnp.float32)


def reference(gate_pre, up_pre, upstream, weight_codes, scales):
    weights = dequantize(weight_codes, scales)
    gate_value = gate_pre.astype(jnp.float32)
    up_value = up_pre.astype(jnp.float32)
    sigmoid_gate = jax.nn.sigmoid(gate_value)
    activated = gate_value * sigmoid_gate
    hidden = (activated * up_value).astype(jnp.bfloat16)
    local_units = FF // N_LOCAL

    def local_part(running, index):
        hidden_cols = lax.dynamic_slice_in_dim(hidden, index * local_units, local_units, 1)
        weight_cols = lax.dynamic_slice_in_dim(weights, index * local_units, local_units, 1)
        partial_term = contract_cols(hidden_cols, weight_cols).astype(jnp.bfloat16)
        partial_term = lax.optimization_barrier(partial_term).astype(jnp.float32)
        return running + partial_term, None

    summed_out, _ = lax.scan(local_part, jnp.zeros((TOKENS, D), jnp.float32), jnp.arange(N_LOCAL, dtype=jnp.int32))
    layer_out = summed_out.astype(jnp.bfloat16)
    back_proj = jnp.dot(upstream, weights, preferred_element_type=jnp.float32)
    gate_grad = (back_proj * up_value * sigmoid_gate * (1.0 + gate_value * (1.0 - sigmoid_gate))).astype(jnp.bfloat16)
    up_grad = (back_proj * activated).astype(jnp.bfloat16)
    groups_total = N_REPLICA * N_NODE
    stacked_up = upstream.reshape(groups_total, TOK_GRP, D)
    stacked_hidden = hidden.reshape(groups_total, TOK_GRP, FF)

    def group_part(running, paired):
        group_term = contract_rows(paired[0], paired[1]).astype(jnp.bfloat16)
        group_term = lax.optimization_barrier(group_term).astype(jnp.float32)
        return running + group_term, None

    grad_total, _ = lax.scan(group_part, jnp.zeros((D, FF), jnp.float32), (stacked_up, stacked_hidden))
    weight_grad = (grad_total / float(N_REPLICA)).astype(jnp.bfloat16)
    return layer_out, gate_grad, up_grad, weight_grad
```

```python
import jax
import jax.numpy as jnp
from jax import lax
from jax.sharding import Mesh, PartitionSpec as P

LINK = jnp.bfloat16


def dequantize(code_rows, scale_rows):
    grouped = code_rows.astype(jnp.float32).reshape(code_rows.shape[0], scale_rows.shape[1], -1)
    scaled = grouped * scale_rows.astype(jnp.float32)[:, :, None]
    return scaled.reshape(code_rows.shape).astype(jnp.bfloat16)


def contract(left, right, left_dim, right_dim):
    return lax.dot_general(
        left, right, (((left_dim,), (right_dim,)), ((), ())), preferred_element_type=jnp.float32
    )


def per_device(gate_pre, up_pre, upstream, weight_codes, scales):
    copies, depth, pairs, cores = (lax.axis_size(name) for name in ("replica", "z", "y", "local"))
    x, z, y, core = (lax.axis_index(name) for name in ("replica", "z", "y", "local"))
    quads = copies * pairs
    offsets = [(dx, dy) for dx in range(copies) for dy in range(pairs)]
    tok_rows, feature_count = upstream.shape
    node_rows, unit_count = weight_codes.shape
    part_units = unit_count // quads
    plane_rows = node_rows * pairs
    owned_rows = feature_count // (copies * depth * pairs)
    core_rows = tok_rows // cores
    block = unit_count // scales.shape[1]

    def place(dx, dy):
        return lax.rem(x + dx + copies, copies) * pairs + lax.rem(y + dy + pairs, pairs)

    def send_plane(value, dx, dy):
        pairs_list = [
            (a * pairs + b, ((a + dx) % copies) * pairs + (b + dy) % pairs)
            for a in range(copies)
            for b in range(pairs)
        ]
        return lax.ppermute(value, ("replica", "y"), pairs_list) if (dx, dy) != (0, 0) else value

    def send_ring(value, axis, size, shift):
        return lax.ppermute(value, axis, [(i, (i + shift) % size) for i in range(size)])

    def send_line(value, shift):
        return lax.ppermute(
            value, "z", [(i, i + shift) for i in range(depth) if 0 <= i + shift < depth]
        )

    def columns(value, index, width):
        return lax.dynamic_slice_in_dim(value, index * width, width, 1)

    def hidden_part(index):
        gate_value = columns(gate_pre, index, part_units).astype(jnp.float32)
        up_value = columns(up_pre, index, part_units).astype(jnp.float32)
        return (gate_value * jax.nn.sigmoid(gate_value) * up_value).astype(jnp.bfloat16)

    def weight_part(index):
        if part_units % block == 0:
            return dequantize(
                columns(weight_codes, index, part_units),
                columns(scales, index, part_units // block),
            )
        return columns(dequantize(weight_codes, scales), index, part_units)

    core_up = lax.dynamic_slice_in_dim(upstream, core * core_rows, core_rows, 0)

    def spread_up(pick):
        along = [pick(z)]
        for shift in range(1, depth):
            along.append(send_ring(pick(lax.rem(z + shift, depth)), "z", depth, shift))
        along = jnp.stack(along)
        around = jnp.stack([send_plane(along, dx, dy) for dx, dy in offsets], axis=1)
        whole = jnp.zeros((depth, quads, cores, core_rows, around.shape[-1]), jnp.bfloat16)
        whole = lax.dynamic_update_slice_in_dim(whole, around[:, :, None], core, 2)
        for shift in range(1, cores):
            whole = lax.dynamic_update_slice_in_dim(
                whole,
                send_ring(around, "local", cores, shift)[:, :, None],
                lax.rem(core - shift + cores, cores),
                2,
            )
        return whole.reshape(depth, quads * tok_rows, around.shape[-1])

    def weight_features(plane):
        return lax.dynamic_slice_in_dim(core_up, plane * plane_rows, plane_rows, 1)

    def grad_features(plane):
        per_copy = pairs * owned_rows
        return jnp.concatenate(
            [
                lax.dynamic_slice_in_dim(core_up, (copy * depth + plane) * per_copy, per_copy, 1)
                for copy in range(copies)
            ],
            axis=1,
        )

    up_weight = spread_up(weight_features)

    groups = [send_plane(hidden_part(place(dx, dy)), dx, dy) for dx, dy in offsets]

    weight = jnp.zeros((pairs, node_rows, part_units), jnp.bfloat16)
    for dy in range(pairs):
        rows = send_plane(weight_part(place(0, dy)), 0, dy)
        weight = lax.dynamic_update_slice_in_dim(
            weight, rows[None], lax.rem(y - dy + pairs, pairs), 0
        )
    weight = weight.reshape(plane_rows, part_units)

    partial = [
        contract(up_weight[k], weight, 1, 0).astype(LINK).reshape(quads, tok_rows, part_units)
        for k in range(depth)
    ]
    partial = jnp.stack(partial)

    above = depth - 1 - z
    received = [[None] * quads for _ in range(depth)]
    back = [None] * quads
    for step in range(quads):
        taken, given = step, quads - 1 - step
        going_up = going_down = groups[taken]
        from_below, from_above = {}, {}

        def own_partial(distance):
            return lax.dynamic_index_in_dim(partial[:, given], distance, 0, keepdims=False)

        for slot in range(1, depth + 1):
            below, over = send_line(going_up, 1), send_line(going_down, -1)
            from_below[slot], from_above[slot] = below, over
            if slot == depth:
                back[given] = (
                    below.astype(jnp.float32) + over.astype(jnp.float32) + own_partial(0).astype(jnp.float32)
                ).astype(LINK)
                break
            goal = jnp.clip(depth - (slot - z), 0, depth - 1)
            mine = own_partial(lax.rem(z - goal + depth, depth))
            going_up = jnp.where(slot <= z, below, below + mine)
            goal = depth - 1 - jnp.clip(depth - (slot - above), 0, depth - 1)
            mine = own_partial(lax.rem(z - goal + depth, depth))
            going_down = jnp.where(slot <= above, over, over + mine)
        received[0][taken] = groups[taken]
        for k in range(1, depth):
            received[k][taken] = jnp.where(k <= z, from_below[k], from_above[depth - k])
    hidden = jnp.concatenate([received[k][o] for k in range(depth) for o in range(quads)], axis=0)

    up_grad_rows = spread_up(grad_features).reshape(depth * quads * tok_rows, plane_rows)
    sums = (contract(up_grad_rows, hidden, 0, 0) / float(copies)).astype(jnp.bfloat16)
    sums = sums.reshape(quads, owned_rows, part_units)
    weight_grad = jnp.zeros((owned_rows, unit_count), jnp.bfloat16)
    for dx, dy in offsets:
        part = send_plane(lax.dynamic_index_in_dim(sums, place(dx, dy), 0, keepdims=False), dx, dy)
        weight_grad = lax.dynamic_update_slice_in_dim(
            weight_grad, part, place(-dx, -dy) * part_units, 1
        )

    gate_grad = jnp.zeros((tok_rows, unit_count), jnp.bfloat16)
    up_grad = jnp.zeros((tok_rows, unit_count), jnp.bfloat16)
    for o, (dx, dy) in enumerate(offsets):
        index = place(dx, dy)
        part = send_plane(back[o], -dx, -dy).astype(jnp.float32)
        gate_value = columns(gate_pre, index, part_units).astype(jnp.float32)
        up_value = columns(up_pre, index, part_units).astype(jnp.float32)
        gate_sig = jax.nn.sigmoid(gate_value)
        gate_part = part * up_value * gate_sig * (1.0 + gate_value * (1.0 - gate_sig))
        up_part = part * gate_value * gate_sig
        start = index * part_units
        gate_grad = lax.dynamic_update_slice_in_dim(gate_grad, gate_part.astype(jnp.bfloat16), start, 1)
        up_grad = lax.dynamic_update_slice_in_dim(up_grad, up_part.astype(jnp.bfloat16), start, 1)

    out = contract(hidden, weight, 1, 1).astype(LINK)
    out = out.reshape(depth, quads, cores, core_rows, plane_rows)
    total = lax.dynamic_index_in_dim(out, core, 2, keepdims=False).astype(jnp.float32)
    for shift in range(1, cores):
        target = lax.rem(core + shift, cores)
        total += send_ring(
            lax.dynamic_index_in_dim(out, target, 2, keepdims=False), "local", cores, shift
        ).astype(jnp.float32)
    total = total.astype(LINK)
    mine = sum(
        send_plane(total[:, o], -dx, -dy).astype(jnp.float32) for o, (dx, dy) in enumerate(offsets)
    ).astype(LINK)
    layer_out = jnp.zeros((core_rows, feature_count), jnp.bfloat16)
    for k in range(depth):
        part = mine[k] if k == 0 else send_ring(mine[k], "z", depth, -k)
        start = lax.rem(z + k, depth) * plane_rows
        layer_out = lax.dynamic_update_slice_in_dim(layer_out, part, start, 1)
    return (layer_out, gate_grad, up_grad, weight_grad)


def solution(mesh):
    copies, nodes, cores = (mesh.shape[name] for name in ("replica", "node", "local"))
    pairs = 2
    inner = Mesh(
        mesh.devices.reshape(copies, nodes // pairs, pairs, cores), ("replica", "z", "y", "local")
    )
    tokens = ("replica", "z", "y")
    in_specs = (
        P(tokens, "local"),
        P(tokens, "local"),
        P(tokens, None),
        P(("z", "y"), "local"),
        P(("z", "y"), "local"),
    )
    out_specs = (
        P(("replica", "z", "y", "local"), None),
        P(tokens, "local"),
        P(tokens, "local"),
        P(tokens, "local"),
    )
    return jax.shard_map(
        per_device, mesh=inner, in_specs=in_specs, out_specs=out_specs, check_vma=False
    )
```

```python
import functools

import jax
import jax.numpy as jnp
from jax import lax
from jax.experimental import pallas as pl
from jax.experimental.pallas import tpu as pltpu
from jax.sharding import Mesh, PartitionSpec as P

LINK = jnp.bfloat16


def contract(left, right, left_dim, right_dim):
    return lax.dot_general(
        left, right, (((left_dim,), (right_dim,)), ((), ())), preferred_element_type=jnp.float32
    )


def after(value, *others):
    return lax.optimization_barrier((value, *others))[0]


def scale_body(block, index_ref, codes_ref, scales_ref, out_ref):
    shape = (scales_ref.shape[1], codes_ref.shape[1])
    unit = lax.broadcasted_iota(jnp.int32, shape, 1) + index_ref[pl.program_id(0)] * shape[1]
    first = lax.broadcasted_iota(jnp.int32, shape, 0) * block
    owned = jnp.where((unit >= first) & (unit < first + block), 1.0, 0.0).astype(jnp.bfloat16)
    spread = jnp.dot(scales_ref[...], owned, preferred_element_type=jnp.float32)
    out_ref[...] = (codes_ref[...].astype(jnp.float32) * spread).astype(jnp.bfloat16)


def dequantize_pieces(codes, scales, indices, piece):
    rows = codes.shape[0]
    block = codes.shape[1] // scales.shape[1]
    if piece % 128 or rows % 256:
        whole = codes.astype(jnp.float32) * jnp.repeat(scales.astype(jnp.float32), block, axis=1)
        return jnp.concatenate(
            [lax.dynamic_slice_in_dim(whole, i * piece, piece, 1) for i in indices], axis=1
        ).astype(jnp.bfloat16)
    count, tile = len(indices), 256
    return pl.pallas_call(
        functools.partial(scale_body, block),
        out_shape=jax.ShapeDtypeStruct((rows, count * piece), jnp.bfloat16),
        grid_spec=pltpu.PrefetchScalarGridSpec(
            num_scalar_prefetch=1,
            grid=(count, rows // tile),
            in_specs=[
                pl.BlockSpec((tile, piece), lambda i, r, index: (r, index[i])),
                pl.BlockSpec((tile, scales.shape[1]), lambda i, r, index: (r, 0)),
            ],
            out_specs=pl.BlockSpec((tile, piece), lambda i, r, index: (r, i)),
        ),
        cost_estimate=pl.CostEstimate(
            flops=rows * count * piece, bytes_accessed=4 * rows * count * piece, transcendentals=0
        ),
    )(jnp.stack(indices).astype(jnp.int32), codes, scales)


def per_device(gate_pre, up_pre, upstream, weight_codes, scales):
    copies, depth, pairs, cores = (lax.axis_size(name) for name in ("replica", "z", "y", "local"))
    x, z, y, core = (lax.axis_index(name) for name in ("replica", "z", "y", "local"))
    above = depth - 1 - z
    tok_rows, feature_count = upstream.shape
    node_rows, unit_count = weight_codes.shape
    halves = 2
    piece = unit_count // (copies * pairs * halves)
    part_units = piece * halves
    chain_units = piece * copies
    plane_rows = node_rows * pairs
    owned_rows = feature_count // (copies * depth * pairs)
    core_rows = tok_rows // cores
    block = unit_count // scales.shape[1]
    group_rows = pairs * tok_rows

    def send_ring(value, axis, size, shift):
        if shift % size == 0:
            return value
        return lax.ppermute(value, axis, [(i, (i + shift) % size) for i in range(size)])

    def send_plane(value, dx, dy):
        moves = [
            (a * pairs + b, ((a + dx) % copies) * pairs + (b + dy) % pairs)
            for a in range(copies)
            for b in range(pairs)
        ]
        return lax.ppermute(value, ("replica", "y"), moves) if (dx, dy) != (0, 0) else value

    def send_lines(up_value, down_value, sources):
        last = depth - 1
        ups = [(i, i + 1) for i in sources]
        downs = [(last - i, last - i - 1) for i in sources]
        ends = {j for _, j in ups}
        apart = not ({i for i, _ in ups} & {i for i, _ in downs}) and not (ends & {j for _, j in downs})
        if not apart:
            return lax.ppermute(up_value, "z", ups), lax.ppermute(down_value, "z", downs)
        first = min(ends)
        if first < depth - first - 1:
            is_up, to_up = z <= max(i for i, _ in ups), z <= max(ends)
        else:
            is_up, to_up = z >= min(i for i, _ in ups), z >= first
        moved = lax.ppermute(jnp.where(is_up, up_value, down_value), "z", ups + downs)
        none = jnp.zeros_like(moved)
        return jnp.where(to_up, moved, none), jnp.where(to_up, none, moved)

    def quarter(dx, dy):
        return lax.rem(y + dy + pairs, pairs) * copies + lax.rem(x + dx + copies, copies)

    def columns(value, index, width):
        return lax.dynamic_slice_in_dim(value, index * width, width, 1)

    near = jnp.minimum(z, above)

    def arrival(j):
        both = j <= 2 * near
        distance = jnp.where(both, (j + 1) // 2, j - near)
        below = jnp.where(both, j % 2 == 1, z > above)
        return distance, below

    def arrival_plane(j):
        distance, below = arrival(j)
        return jnp.where(below, z - distance, z + distance)

    def arrival_index(plane):
        distance = jnp.abs(plane - z)
        return jnp.where(
            distance <= near, 2 * distance - (plane < z).astype(jnp.int32), near + distance
        )

    core_up = lax.dynamic_slice_in_dim(upstream, core * core_rows, core_rows, 0)

    def plane_features(plane):
        per_copy = pairs * owned_rows
        return jnp.concatenate(
            [lax.dynamic_slice_in_dim(core_up, plane * plane_rows, plane_rows, 1)]
            + [
                lax.dynamic_slice_in_dim(core_up, (copy * depth + plane) * per_copy, per_copy, 1)
                for copy in range(copies)
            ],
            axis=1,
        )

    along = [plane_features(z)]
    for shift in range(1, depth):
        along.append(send_ring(plane_features(lax.rem(z + shift, depth)), "z", depth, shift))
    along = jnp.stack(along)

    def hidden_part(dy):
        parts = []
        for h in range(halves):
            for dx in range(copies):
                index = quarter(dx, dy) * halves + h
                gate_value = columns(gate_pre, index, piece).astype(jnp.float32)
                up_value = columns(up_pre, index, piece).astype(jnp.float32)
                parts.append((gate_value * jax.nn.sigmoid(gate_value) * up_value).astype(jnp.bfloat16))
        return jnp.concatenate(parts, axis=1)

    groups = [send_ring(hidden_part(dy), "y", pairs, dy) for dy in range(pairs)]

    def weight_parts(places, h, codes):
        return dequantize_pieces(codes, scales, [quarter(dx, dy) * halves + h for dx, dy in places], piece)

    given = [[weight_parts([(0, dy)], h, weight_codes) for dy in range(1, pairs)] for h in range(halves)]
    direct = [[send_ring(part, "y", pairs, dy + 1) for dy, part in enumerate(given[0])]]

    up_own = after(along[:, :, :plane_rows], groups[1], direct[0][0])
    around = [send_ring(up_own, "y", pairs, dy) for dy in range(pairs)]
    for h in range(1, halves):
        direct.append([send_ring(after(part, around[1]), "y", pairs, dy + 1) for dy, part in enumerate(given[h])])
    rows = []
    for h in range(halves):
        codes = after(weight_codes, along)
        rows_h = [weight_parts([(dx, 0) for dx in range(copies)], h, codes)]
        for dy in range(1, pairs):
            passed = [direct[h][dy - 1]]
            passed += [send_ring(passed[0], "replica", copies, -dx) for dx in range(1, copies)]
            rows_h.append(jnp.concatenate(passed, axis=1))
        rows.append(rows_h)

    steps = [[(after(group, along),) * 2] for group in groups]
    for step in range(1, depth):
        for chain in steps:
            chain.append(send_lines(*chain[-1], range(step - 1, depth - 1)))

    around = after(jnp.stack(around, axis=1), *steps[0][1])
    whole = jnp.zeros((depth, pairs, cores, core_rows, plane_rows), jnp.bfloat16)
    for shift in range(cores):
        whole = lax.dynamic_update_slice_in_dim(
            whole,
            send_ring(around, "local", cores, shift)[:, :, None],
            lax.rem(core - shift + cores, cores),
            2,
        )
    up_weight = whole.reshape(depth * group_rows, plane_rows)

    weight, partial = [], []
    for h in range(halves):
        first = jnp.where(y == 0, rows[h][0], rows[h][1]) if pairs == 2 else None
        second = jnp.where(y == 0, rows[h][1], rows[h][0])
        weight.append(jnp.concatenate([first, second], axis=0))
        ready = after(up_weight, *(steps[1][1] if h == 0 else steps[0][2]))
        product = contract(ready, weight[h], 1, 0).astype(LINK)
        partial.append(product.reshape(depth, group_rows, chain_units))

    def own_partial(h, goal):
        return lax.dynamic_index_in_dim(
            partial[h], lax.rem(z - goal + depth, depth), 0, keepdims=False
        )

    sums = [(jnp.zeros((), LINK), jnp.zeros((), LINK)) for _ in range(halves)]
    for step in range(1, depth):
        for h in range(halves):
            if depth == 4 and step > 1:
                sums[h] = after(sums[h], *{(2, 0): steps[1][2], (2, 1): steps[0][3], (3, 0): steps[1][3], (3, 1): ()}[step, h])
            goal = jnp.clip(depth - step + z, 0, depth - 1)
            going_up = sums[h][0] + own_partial(h, goal)
            goal = jnp.clip(step + z - depth, 0, depth - 1)
            going_down = sums[h][1] + own_partial(h, goal)
            sums[h] = send_lines(going_up, going_down, range(step))
    arrived = [jnp.concatenate(groups, axis=0)]
    for j in range(1, depth):
        distance, below = arrival(j)
        chosen = []
        for chain in steps:
            value = None
            for d in range((j + 1) // 2, j + 1):
                pick = jnp.where(below, chain[d][0], chain[d][1])
                value = pick if value is None else jnp.where(distance == d, pick, value)
            chosen.append(value)
        arrived.append(jnp.concatenate(chosen, axis=0))

    def of_quarter(value, dx):
        return jnp.concatenate(
            [value[:, (h * copies + dx) * piece : (h * copies + dx + 1) * piece] for h in range(halves)], axis=1
        )

    quartered = []
    for j in range(depth):
        for dx in range(copies):
            quartered.append(send_ring(of_quarter(arrived[j], dx), "replica", copies, dx))
    hidden = jnp.concatenate(arrived, axis=0)
    hidden_quarter = jnp.concatenate(quartered, axis=0)

    out = contract(hidden, jnp.concatenate(weight, axis=1), 1, 1).astype(LINK)
    out = out.reshape(depth, pairs, cores, core_rows, plane_rows)
    total = lax.dynamic_index_in_dim(out, core, 2, keepdims=False).astype(jnp.float32)
    for shift in range(1, cores):
        target = lax.rem(core + shift, cores)
        total += send_ring(
            lax.dynamic_index_in_dim(out, target, 2, keepdims=False), "local", cores, shift
        ).astype(jnp.float32)
    total = total.astype(LINK)
    mine = sum(send_ring(total[:, g], "y", pairs, -g).astype(jnp.float32) for g in range(pairs)).astype(LINK)
    layer_out = jnp.zeros((core_rows, feature_count), jnp.bfloat16)
    for k in range(depth):
        plane = lax.rem(z - k + depth, depth)
        part = lax.dynamic_index_in_dim(mine, arrival_index(plane), 0, keepdims=False)
        part = send_ring(part, "z", depth, -k)
        layer_out = lax.dynamic_update_slice_in_dim(
            layer_out, part, lax.rem(z + k, depth) * plane_rows, 1
        )

    up_sums = after(along[:, :, plane_rows:], partial[halves - 1])
    up_sums = jnp.stack([send_ring(up_sums, "y", pairs, dy) for dy in range(pairs)], axis=1)
    up_sums = jnp.stack([send_ring(up_sums, "replica", copies, dx) for dx in range(copies)], axis=1)
    whole = jnp.zeros((depth, copies, pairs, cores, core_rows, plane_rows), jnp.bfloat16)
    for shift in range(cores):
        whole = lax.dynamic_update_slice_in_dim(
            whole,
            send_ring(up_sums, "local", cores, shift)[:, :, :, None],
            lax.rem(core - shift + cores, cores),
            3,
        )
    up_sums = jnp.concatenate(
        [
            lax.dynamic_index_in_dim(whole, lax.rem(z - arrival_plane(j) + depth, depth), 0, keepdims=False)
            for j in range(depth)
        ]
    ).reshape(-1, plane_rows)
    grads = (contract(up_sums, hidden_quarter, 0, 0) / float(copies)).astype(jnp.bfloat16)
    grads = grads.reshape(copies * pairs, owned_rows, part_units)
    weight_grad = jnp.zeros((owned_rows, unit_count), jnp.bfloat16)
    for dx in range(copies):
        for dy in range(pairs):
            chip = lax.rem(x + dx, copies) * pairs + lax.rem(y + dy, pairs)
            part = send_plane(lax.dynamic_index_in_dim(grads, chip, 0, keepdims=False), dx, dy)
            weight_grad = lax.dynamic_update_slice_in_dim(
                weight_grad, part, quarter(-dx, -dy) * part_units, 1
            )

    sums[0] = after(sums[0], grads)
    back = []
    for h in range(halves):
        total = sum(v.astype(jnp.float32) for v in (*sums[h], own_partial(h, z)))
        back.append(total.astype(LINK).reshape(pairs, tok_rows, chain_units))

    gate_grad = jnp.zeros((tok_rows, unit_count), jnp.bfloat16)
    up_grad = jnp.zeros((tok_rows, unit_count), jnp.bfloat16)
    for h in range(halves):
        for g in range(pairs):
            whole_part = send_ring(back[h][g], "y", pairs, -g)
            for dx in range(copies):
                index = quarter(dx, g) * halves + h
                part = whole_part[:, dx * piece : (dx + 1) * piece].astype(jnp.float32)
                gate_value = columns(gate_pre, index, piece).astype(jnp.float32)
                up_value = columns(up_pre, index, piece).astype(jnp.float32)
                gate_sig = jax.nn.sigmoid(gate_value)
                gate_part = part * up_value * gate_sig * (1.0 + gate_value * (1.0 - gate_sig))
                up_part = part * gate_value * gate_sig
                start = index * piece
                gate_grad = lax.dynamic_update_slice_in_dim(gate_grad, gate_part.astype(jnp.bfloat16), start, 1)
                up_grad = lax.dynamic_update_slice_in_dim(up_grad, up_part.astype(jnp.bfloat16), start, 1)
    return (layer_out, gate_grad, up_grad, weight_grad)


def solution(mesh):
    copies, nodes, cores = (mesh.shape[name] for name in ("replica", "node", "local"))
    pairs = 2
    inner = Mesh(
        mesh.devices.reshape(copies, nodes // pairs, pairs, cores), ("replica", "z", "y", "local")
    )
    tokens = ("replica", "z", "y")
    in_specs = (
        P(tokens, "local"),
        P(tokens, "local"),
        P(tokens, None),
        P(("z", "y"), "local"),
        P(("z", "y"), "local"),
    )
    out_specs = (
        P(("replica", "z", "y", "local"), None),
        P(tokens, "local"),
        P(tokens, "local"),
        P(tokens, "local"),
    )
    return jax.shard_map(
        per_device, mesh=inner, in_specs=in_specs, out_specs=out_specs, check_vma=False
    )
```

```python
import functools

import jax
import jax.numpy as jnp
from jax import lax
from jax.experimental import pallas as pl
from jax.experimental.pallas import tpu as pltpu
from jax.sharding import Mesh, PartitionSpec as P

LINK = jnp.bfloat16


def contract(left, right, left_dim, right_dim):
    return lax.dot_general(
        left, right, (((left_dim,), (right_dim,)), ((), ())), preferred_element_type=jnp.float32
    )


def project_body(steps, left_ref, *refs):
    *right_refs, out_ref, total_ref = refs
    step = pl.program_id(1)

    @pl.when(step == 0)
    def _():
        total_ref[...] = jnp.zeros_like(total_ref)

    for h, right_ref in enumerate(right_refs):

        @pl.when(lax.div(step, steps) == h)
        def _(right_ref=right_ref):
            total_ref[...] += contract(left_ref[...], right_ref[...], 1, 1)

    @pl.when(step == pl.num_programs(1) - 1)
    def _():
        out_ref[...] = total_ref[...].astype(out_ref.dtype)


def project(left, rights):
    rows = left.shape[0]
    columns, width = rights[0].shape
    row_tile, tile = 512, width // 2
    if tile % 128 or rows % row_tile or columns % 128:
        return contract(left, jnp.concatenate(rights, axis=1), 1, 1).astype(LINK)
    steps = width // tile
    flops = 2 * rows * columns * width * len(rights)
    return pl.pallas_call(
        functools.partial(project_body, steps),
        out_shape=jax.ShapeDtypeStruct((rows, columns), LINK),
        grid=(rows // row_tile, steps * len(rights)),
        in_specs=[pl.BlockSpec((row_tile, tile), lambda i, k: (i, k))]
        + [
            pl.BlockSpec((columns, tile), lambda i, k, h=h: (0, jnp.clip(k - h * steps, 0, steps - 1)))
            for h in range(len(rights))
        ],
        out_specs=pl.BlockSpec((row_tile, columns), lambda i, k: (i, 0)),
        scratch_shapes=[pltpu.VMEM((row_tile, columns), jnp.float32)],
        cost_estimate=pl.CostEstimate(flops=flops, bytes_accessed=flops // 256, transcendentals=0),
        compiler_params=pltpu.CompilerParams(vmem_limit_bytes=24 * 1024 * 1024),
    )(left, *rights)


def after(value, *others):
    return lax.optimization_barrier((value, *others))[0]


def scale_body(block, index_ref, codes_ref, scales_ref, out_ref):
    shape = (scales_ref.shape[1], codes_ref.shape[1])
    unit = lax.broadcasted_iota(jnp.int32, shape, 1) + index_ref[pl.program_id(0)] * shape[1]
    first = lax.broadcasted_iota(jnp.int32, shape, 0) * block
    owned = jnp.where((unit >= first) & (unit < first + block), 1.0, 0.0).astype(jnp.bfloat16)
    spread = jnp.dot(scales_ref[...], owned, preferred_element_type=jnp.float32)
    out_ref[...] = (codes_ref[...].astype(jnp.float32) * spread).astype(jnp.bfloat16)


def dequantize_pieces(codes, scales, indices, piece):
    rows = codes.shape[0]
    block = codes.shape[1] // scales.shape[1]
    if piece % 128 or rows % 256:
        whole = codes.astype(jnp.float32) * jnp.repeat(scales.astype(jnp.float32), block, axis=1)
        return jnp.concatenate(
            [lax.dynamic_slice_in_dim(whole, i * piece, piece, 1) for i in indices], axis=1
        ).astype(jnp.bfloat16)
    count, tile = len(indices), 256
    return pl.pallas_call(
        functools.partial(scale_body, block),
        out_shape=jax.ShapeDtypeStruct((rows, count * piece), jnp.bfloat16),
        grid_spec=pltpu.PrefetchScalarGridSpec(
            num_scalar_prefetch=1,
            grid=(count, rows // tile),
            in_specs=[
                pl.BlockSpec((tile, piece), lambda i, r, index: (r, index[i])),
                pl.BlockSpec((tile, scales.shape[1]), lambda i, r, index: (r, 0)),
            ],
            out_specs=pl.BlockSpec((tile, piece), lambda i, r, index: (r, i)),
        ),
        cost_estimate=pl.CostEstimate(
            flops=rows * count * piece, bytes_accessed=4 * rows * count * piece, transcendentals=0
        ),
    )(jnp.stack(indices).astype(jnp.int32), codes, scales)


def per_device(gate_pre, up_pre, upstream, weight_codes, scales):
    copies, depth, pairs, cores = (lax.axis_size(name) for name in ("replica", "z", "y", "local"))
    x, z, y, core = (lax.axis_index(name) for name in ("replica", "z", "y", "local"))
    above = depth - 1 - z
    tok_rows, feature_count = upstream.shape
    node_rows, unit_count = weight_codes.shape
    halves = 2
    piece = unit_count // (copies * pairs * halves)
    part_units = piece * halves
    chain_units = piece * copies
    plane_rows = node_rows * pairs
    owned_rows = feature_count // (copies * depth * pairs)
    core_rows = tok_rows // cores
    block = unit_count // scales.shape[1]
    group_rows = pairs * tok_rows

    def send_ring(value, axis, size, shift):
        if shift % size == 0:
            return value
        return lax.ppermute(value, axis, [(i, (i + shift) % size) for i in range(size)])

    def send_plane(value, dx, dy):
        moves = [
            (a * pairs + b, ((a + dx) % copies) * pairs + (b + dy) % pairs)
            for a in range(copies)
            for b in range(pairs)
        ]
        return lax.ppermute(value, ("replica", "y"), moves) if (dx, dy) != (0, 0) else value

    def send_lines(up_value, down_value, sources):
        last = depth - 1
        ups = [(i, i + 1) for i in sources]
        downs = [(last - i, last - i - 1) for i in sources]
        ends = {j for _, j in ups}
        apart = not ({i for i, _ in ups} & {i for i, _ in downs}) and not (ends & {j for _, j in downs})
        if not apart:
            return lax.ppermute(up_value, "z", ups), lax.ppermute(down_value, "z", downs)
        first = min(ends)
        if first < depth - first - 1:
            is_up, to_up = z <= max(i for i, _ in ups), z <= max(ends)
        else:
            is_up, to_up = z >= min(i for i, _ in ups), z >= first
        moved = lax.ppermute(jnp.where(is_up, up_value, down_value), "z", ups + downs)
        none = jnp.zeros_like(moved)
        return jnp.where(to_up, moved, none), jnp.where(to_up, none, moved)

    def quarter(dx, dy):
        return lax.rem(y + dy + pairs, pairs) * copies + lax.rem(x + dx + copies, copies)

    def columns(value, index, width):
        return lax.dynamic_slice_in_dim(value, index * width, width, 1)

    def of_quarter(value, dx):
        return jnp.concatenate(
            [value[:, (h * copies + dx) * piece : (h * copies + dx + 1) * piece] for h in range(halves)], axis=1
        )

    near = jnp.minimum(z, above)

    def arrival(j):
        both = j <= 2 * near
        distance = jnp.where(both, (j + 1) // 2, j - near)
        below = jnp.where(both, j % 2 == 1, z > above)
        return distance, below

    def arrival_plane(j):
        distance, below = arrival(j)
        return jnp.where(below, z - distance, z + distance)

    def arrival_index(plane):
        distance = jnp.abs(plane - z)
        return jnp.where(
            distance <= near, 2 * distance - (plane < z).astype(jnp.int32), near + distance
        )

    def hidden_part(dy):
        parts = []
        for h in range(halves):
            for dx in range(copies):
                index = quarter(dx, dy) * halves + h
                gate_value = columns(gate_pre, index, piece).astype(jnp.float32)
                up_value = columns(up_pre, index, piece).astype(jnp.float32)
                parts.append((gate_value * jax.nn.sigmoid(gate_value) * up_value).astype(jnp.bfloat16))
        return jnp.concatenate(parts, axis=1)

    hidden_parts = [hidden_part(dy) for dy in range(pairs)]
    groups = [send_ring(part, "y", pairs, dy) for dy, part in enumerate(hidden_parts)]

    core_up = lax.dynamic_slice_in_dim(after(upstream, *hidden_parts[1:]), core * core_rows, core_rows, 0)

    def plane_features(plane):
        per_copy = pairs * owned_rows
        return jnp.concatenate(
            [lax.dynamic_slice_in_dim(core_up, plane * plane_rows, plane_rows, 1)]
            + [
                lax.dynamic_slice_in_dim(core_up, (copy * depth + plane) * per_copy, per_copy, 1)
                for copy in range(copies)
            ],
            axis=1,
        )

    along = [plane_features(z)]
    for shift in range(1, depth):
        along.append(send_ring(plane_features(lax.rem(z + shift, depth)), "z", depth, shift))
    along = jnp.stack(along)

    def weight_parts(places, h, codes):
        return dequantize_pieces(codes, scales, [quarter(dx, dy) * halves + h for dx, dy in places], piece)

    given = [[weight_parts([(0, dy)], h, weight_codes) for dy in range(1, pairs)] for h in range(halves)]
    own = [weight_parts([(dx, 0) for dx in range(copies)], h, after(weight_codes, given[0][0])) for h in range(halves)]
    early = send_lines(*(after(groups[0], along),) * 2, range(depth - 1))
    groups = [groups[0]] + after(groups[1:], *own, *given[1])
    steps = [(jnp.concatenate(groups, axis=0),) * 2]

    up_own = along[:, :, :plane_rows]
    rows = []
    for h in range(halves):
        rows_h = [own[h]]
        for dy in range(1, pairs):
            ready = after(given[h][dy - 1], *([around[1]] if h else []))
            ready = send_ring(ready, "y", pairs, dy)
            if h == 0:
                ready = after(ready, steps[0][0])
                up_own = after(up_own, ready)
                around = [send_ring(up_own, "y", pairs, shift) for shift in range(pairs)]
            passed = [ready] + [send_ring(ready, "replica", copies, -dx) for dx in range(1, copies)]
            rows_h.append(jnp.concatenate(passed, axis=1))
        rows.append(rows_h)

    late = [send_lines(group, group, range(depth - 1)) for group in after(groups[1:], *early)]
    steps.append(tuple(jnp.concatenate([early[side]] + [v[side] for v in late], axis=0) for side in range(2)))
    for step in range(2, depth):
        steps.append(send_lines(*steps[-1], range(step - 1, depth - 1)))

    around = jnp.stack(around, axis=1)
    whole = jnp.zeros((depth, pairs, cores, core_rows, plane_rows), jnp.bfloat16)
    for shift in range(cores):
        whole = lax.dynamic_update_slice_in_dim(
            whole,
            send_ring(around, "local", cores, shift)[:, :, None],
            lax.rem(core - shift + cores, cores),
            2,
        )
    up_weight = whole.reshape(depth * group_rows, plane_rows)

    weight, partial = [], []
    for h in range(halves):
        first = jnp.where(y == 0, rows[h][0], rows[h][1]) if pairs == 2 else None
        second = jnp.where(y == 0, rows[h][1], rows[h][0])
        weight.append(jnp.concatenate([first, second], axis=0))
        product = contract(up_weight if h else after(up_weight, *steps[1]), weight[h], 1, 0).astype(LINK)
        partial.append(product.reshape(depth, group_rows, chain_units))

    up_sums = after(along[:, :, plane_rows:], rows[0][1])
    up_sums = jnp.stack([send_ring(up_sums, "replica", copies, dx) for dx in range(copies)], axis=1)
    up_sums = jnp.stack([send_ring(up_sums, "y", pairs, dy) for dy in range(pairs)], axis=2)


    arrived = [steps[0][0]]
    for j in range(1, depth):
        distance, below = arrival(j)
        value = None
        for d in range((j + 1) // 2, j + 1):
            came = after(steps[d], arrived[j - 1])
            pick = jnp.where(below, came[0], came[1])
            value = pick if value is None else jnp.where(distance == d, pick, value)
        arrived.append(value)

    crossed = []
    for j in range(depth):
        ready = after(arrived[j], rows[1][1], partial[0])
        crossed.append([send_ring(of_quarter(ready, dx), "replica", copies, dx) for dx in range(copies)])
    hidden_quarter = jnp.concatenate([part for parts in crossed for part in parts], axis=0)

    up_sums = after(up_sums, *steps[depth - 1])
    whole = jnp.zeros((depth, copies, pairs, cores, core_rows, plane_rows), jnp.bfloat16)
    for shift in range(cores):
        whole = lax.dynamic_update_slice_in_dim(
            whole,
            send_ring(up_sums, "local", cores, shift)[:, :, :, None],
            lax.rem(core - shift + cores, cores),
            3,
        )
    up_sums = jnp.concatenate(
        [
            lax.dynamic_index_in_dim(whole, lax.rem(z - arrival_plane(j) + depth, depth), 0, keepdims=False)
            for j in range(depth)
        ]
    ).reshape(-1, plane_rows)

    def own_partial(goal):
        index = lax.rem(z - goal + depth, depth)
        return [lax.dynamic_index_in_dim(part, index, 0, keepdims=False) for part in partial]

    goals = [(jnp.clip(depth - step + z, 0, depth - 1), jnp.clip(step + z - depth, 0, depth - 1)) for step in range(depth)]
    first = own_partial(jnp.where(2 * z < depth, *goals[1]))
    first = [send_lines(value, value, range(1)) for value in first]
    sums = [jnp.concatenate([v[side] for v in first], axis=1) for side in range(2)]
    for step in range(2, depth):
        if step == depth - 2:
            sums = after(sums, *crossed[1], *steps[depth - 2])
        going = [jnp.concatenate(own_partial(goals[step][side]), axis=1) + sums[side] for side in range(2)]
        if step < depth - 1:
            sums = send_lines(*going, range(step))

    out = project(after(jnp.concatenate(arrived, axis=0)), weight)
    out = out.reshape(depth, pairs, cores, core_rows, plane_rows)
    total = lax.dynamic_index_in_dim(out, core, 2, keepdims=False).astype(jnp.float32)
    for shift in range(1, cores):
        target = lax.rem(core + shift, cores)
        total += send_ring(
            lax.dynamic_index_in_dim(out, target, 2, keepdims=False), "local", cores, shift
        ).astype(jnp.float32)
    total = total.astype(LINK)
    mine = sum(send_ring(total[:, g], "y", pairs, -g).astype(jnp.float32) for g in range(pairs)).astype(LINK)

    grads = (contract(up_sums, after(hidden_quarter), 0, 0) / float(copies)).astype(jnp.bfloat16)

    sums = []
    for h in range(halves):
        part = [value[:, h * chain_units : (h + 1) * chain_units] for value in going]
        sums.append(send_lines(*after(part, *((*sums[0], grads) if h else (out,))), range(depth - 1)))

    grads = after(grads, mine, *sums[0]).reshape(copies * pairs, owned_rows, part_units)
    weight_grad = jnp.zeros((owned_rows, unit_count), jnp.bfloat16)
    for dx in range(copies):
        for dy in range(pairs):
            chip = lax.rem(x + dx, copies) * pairs + lax.rem(y + dy, pairs)
            part = send_plane(lax.dynamic_index_in_dim(grads, chip, 0, keepdims=False), dx, dy)
            weight_grad = lax.dynamic_update_slice_in_dim(
                weight_grad, part, quarter(-dx, -dy) * part_units, 1
            )

    own_sums = own_partial(z)
    returned = []
    for h in range(halves):
        total = sum(v.astype(jnp.float32) for v in (*sums[h], own_sums[h]))
        back = total.astype(LINK).reshape(pairs, tok_rows, chain_units)
        returned.append([send_ring(back[g], "y", pairs, -g) for g in range(pairs)])

    mine = after(mine, *sums[1])
    layer_out = jnp.zeros((core_rows, feature_count), jnp.bfloat16)
    for k in range(depth):
        plane = lax.rem(z - k + depth, depth)
        part = lax.dynamic_index_in_dim(mine, arrival_index(plane), 0, keepdims=False)
        part = send_ring(part, "z", depth, -k)
        layer_out = lax.dynamic_update_slice_in_dim(
            layer_out, part, lax.rem(z + k, depth) * plane_rows, 1
        )

    gate_grad = jnp.zeros((tok_rows, unit_count), jnp.bfloat16)
    up_grad = jnp.zeros((tok_rows, unit_count), jnp.bfloat16)
    for g in range(pairs):
        for h in range(halves):
            whole_part = returned[h][g]
            for dx in range(copies):
                index = quarter(dx, g) * halves + h
                part = whole_part[:, dx * piece : (dx + 1) * piece].astype(jnp.float32)
                gate_value = columns(gate_pre, index, piece).astype(jnp.float32)
                up_value = columns(up_pre, index, piece).astype(jnp.float32)
                gate_sig = jax.nn.sigmoid(gate_value)
                gate_part = part * up_value * gate_sig * (1.0 + gate_value * (1.0 - gate_sig))
                up_part = part * gate_value * gate_sig
                start = index * piece
                gate_grad = lax.dynamic_update_slice_in_dim(gate_grad, gate_part.astype(jnp.bfloat16), start, 1)
                up_grad = lax.dynamic_update_slice_in_dim(up_grad, up_part.astype(jnp.bfloat16), start, 1)
    return (layer_out, gate_grad, up_grad, weight_grad)


def solution(mesh):
    copies, nodes, cores = (mesh.shape[name] for name in ("replica", "node", "local"))
    pairs = 2
    inner = Mesh(
        mesh.devices.reshape(copies, nodes // pairs, pairs, cores), ("replica", "z", "y", "local")
    )
    tokens = ("replica", "z", "y")
    in_specs = (
        P(tokens, "local"),
        P(tokens, "local"),
        P(tokens, None),
        P(("z", "y"), "local"),
        P(("z", "y"), "local"),
    )
    out_specs = (
        P(("replica", "z", "y", "local"), None),
        P(tokens, "local"),
        P(tokens, "local"),
        P(tokens, "local"),
    )
    return jax.shard_map(
        per_device, mesh=inner, in_specs=in_specs, out_specs=out_specs, check_vma=False
    )
```

```python
import functools

import jax
import jax.numpy as jnp
from jax import lax
from jax.experimental import pallas as pl
from jax.experimental.pallas import tpu as pltpu
from jax.sharding import Mesh, PartitionSpec as P

LINK = jnp.bfloat16


def contract(left, right, left_dim, right_dim):
    return lax.dot_general(
        left, right, (((left_dim,), (right_dim,)), ((), ())), preferred_element_type=jnp.float32
    )


def project_body(steps, left_ref, *refs):
    *right_refs, out_ref, total_ref = refs
    step = pl.program_id(1)

    @pl.when(step == 0)
    def _():
        total_ref[...] = jnp.zeros_like(total_ref)

    for h, right_ref in enumerate(right_refs):

        @pl.when(lax.div(step, steps) == h)
        def _(right_ref=right_ref):
            total_ref[...] += contract(left_ref[...], right_ref[...], 1, 1)

    @pl.when(step == pl.num_programs(1) - 1)
    def _():
        out_ref[...] = total_ref[...].astype(out_ref.dtype)


def project(left, rights):
    rows = left.shape[0]
    columns, width = rights[0].shape
    row_tile, tile = 512, width // 2
    if tile % 128 or rows % row_tile or columns % 128:
        return contract(left, jnp.concatenate(rights, axis=1), 1, 1).astype(LINK)
    steps = width // tile
    flops = 2 * rows * columns * width * len(rights)
    return pl.pallas_call(
        functools.partial(project_body, steps),
        out_shape=jax.ShapeDtypeStruct((rows, columns), LINK),
        grid=(rows // row_tile, steps * len(rights)),
        in_specs=[pl.BlockSpec((row_tile, tile), lambda i, k: (i, k))]
        + [
            pl.BlockSpec((columns, tile), lambda i, k, h=h: (0, jnp.clip(k - h * steps, 0, steps - 1)))
            for h in range(len(rights))
        ],
        out_specs=pl.BlockSpec((row_tile, columns), lambda i, k: (i, 0)),
        scratch_shapes=[pltpu.VMEM((row_tile, columns), jnp.float32)],
        cost_estimate=pl.CostEstimate(flops=flops, bytes_accessed=flops // 256, transcendentals=0),
        compiler_params=pltpu.CompilerParams(vmem_limit_bytes=24 * 1024 * 1024),
    )(left, *rights)


def after(value, *others):
    return lax.optimization_barrier((value, *others))[0]


def scale_body(block, index_ref, codes_ref, scales_ref, out_ref):
    shape = (scales_ref.shape[1], codes_ref.shape[1])
    unit = lax.broadcasted_iota(jnp.int32, shape, 1) + index_ref[pl.program_id(0)] * shape[1]
    first = lax.broadcasted_iota(jnp.int32, shape, 0) * block
    owned = jnp.where((unit >= first) & (unit < first + block), 1.0, 0.0).astype(jnp.bfloat16)
    spread = jnp.dot(scales_ref[...], owned, preferred_element_type=jnp.float32)
    out_ref[...] = (codes_ref[...].astype(jnp.float32) * spread).astype(jnp.bfloat16)


def dequantize_pieces(codes, scales, indices, piece, slots=1, slot=0):
    rows = codes.shape[0]
    block = codes.shape[1] // scales.shape[1]
    if piece % 128 or rows % 256:
        whole = codes.astype(jnp.float32) * jnp.repeat(scales.astype(jnp.float32), block, axis=1)
        parts = [lax.dynamic_slice_in_dim(whole, i * piece, piece, 1) for i in indices]
        parts = jnp.concatenate(parts, axis=1).astype(jnp.bfloat16)
        return lax.dynamic_update_slice_in_dim(
            jnp.zeros((slots * rows, parts.shape[1]), jnp.bfloat16), parts, slot * rows, 0
        )
    count, tile = len(indices), 256
    return pl.pallas_call(
        functools.partial(scale_body, block),
        out_shape=jax.ShapeDtypeStruct((slots * rows, count * piece), jnp.bfloat16),
        grid_spec=pltpu.PrefetchScalarGridSpec(
            num_scalar_prefetch=1,
            grid=(count, rows // tile),
            in_specs=[
                pl.BlockSpec((tile, piece), lambda i, r, index: (r, index[i])),
                pl.BlockSpec((tile, scales.shape[1]), lambda i, r, index: (r, 0)),
            ],
            out_specs=pl.BlockSpec(
                (tile, piece), lambda i, r, index: (index[count] * (rows // tile) + r, i)
            ),
        ),
        cost_estimate=pl.CostEstimate(
            flops=rows * count * piece, bytes_accessed=4 * rows * count * piece, transcendentals=0
        ),
    )(jnp.stack([*indices, jnp.asarray(slot)]).astype(jnp.int32), codes, scales)


def per_device(gate_pre, up_pre, upstream, weight_codes, scales):
    copies, depth, pairs, cores = (lax.axis_size(name) for name in ("replica", "z", "y", "local"))
    x, z, y, core = (lax.axis_index(name) for name in ("replica", "z", "y", "local"))
    above = depth - 1 - z
    tok_rows, feature_count = upstream.shape
    node_rows, unit_count = weight_codes.shape
    halves = 2
    piece = unit_count // (copies * pairs * halves)
    part_units = piece * halves
    chain_units = piece * copies
    plane_rows = node_rows * pairs
    owned_rows = feature_count // (copies * depth * pairs)
    core_rows = tok_rows // cores
    block = unit_count // scales.shape[1]
    group_rows = pairs * tok_rows

    def send_ring(value, axis, size, shift):
        if shift % size == 0:
            return value
        return lax.ppermute(value, axis, [(i, (i + shift) % size) for i in range(size)])

    def send_plane(value, dx, dy):
        moves = [
            (a * pairs + b, ((a + dx) % copies) * pairs + (b + dy) % pairs)
            for a in range(copies)
            for b in range(pairs)
        ]
        return lax.ppermute(value, ("replica", "y"), moves) if (dx, dy) != (0, 0) else value

    def send_lines(up_value, down_value, sources):
        last = depth - 1
        ups = [(i, i + 1) for i in sources]
        downs = [(last - i, last - i - 1) for i in sources]
        ends = {j for _, j in ups}
        apart = not ({i for i, _ in ups} & {i for i, _ in downs}) and not (ends & {j for _, j in downs})
        if not apart:
            return lax.ppermute(up_value, "z", ups), lax.ppermute(down_value, "z", downs)
        first = min(ends)
        if first < depth - first - 1:
            is_up, to_up = z <= max(i for i, _ in ups), z <= max(ends)
        else:
            is_up, to_up = z >= min(i for i, _ in ups), z >= first
        moved = lax.ppermute(jnp.where(is_up, up_value, down_value), "z", ups + downs)
        none = jnp.zeros_like(moved)
        return jnp.where(to_up, moved, none), jnp.where(to_up, none, moved)

    def quarter(dx, dy):
        return lax.rem(y + dy + pairs, pairs) * copies + lax.rem(x + dx + copies, copies)

    def columns(value, index, width):
        return lax.dynamic_slice_in_dim(value, index * width, width, 1)

    def of_quarter(value, dx):
        return jnp.concatenate(
            [value[:, (h * copies + dx) * piece : (h * copies + dx + 1) * piece] for h in range(halves)], axis=1
        )

    near = jnp.minimum(z, above)

    def arrival(j):
        both = j <= 2 * near
        distance = jnp.where(both, (j + 1) // 2, j - near)
        below = jnp.where(both, j % 2 == 1, z > above)
        return distance, below

    def arrival_plane(j):
        distance, below = arrival(j)
        return jnp.where(below, z - distance, z + distance)

    def arrival_index(plane):
        distance = jnp.abs(plane - z)
        return jnp.where(
            distance <= near, 2 * distance - (plane < z).astype(jnp.int32), near + distance
        )

    def hidden_part(dy):
        parts = []
        for h in range(halves):
            for dx in range(copies):
                index = quarter(dx, dy) * halves + h
                gate_value = columns(gate_pre, index, piece).astype(jnp.float32)
                up_value = columns(up_pre, index, piece).astype(jnp.float32)
                parts.append((gate_value * jax.nn.sigmoid(gate_value) * up_value).astype(jnp.bfloat16))
        return jnp.concatenate(parts, axis=1)

    hidden_parts = [hidden_part(dy) for dy in range(pairs)]
    groups = [send_ring(part, "y", pairs, dy) for dy, part in enumerate(hidden_parts)]

    core_up = lax.dynamic_slice_in_dim(after(upstream, *hidden_parts[1:]), core * core_rows, core_rows, 0)

    def plane_features(plane):
        per_copy = pairs * owned_rows
        return jnp.concatenate(
            [lax.dynamic_slice_in_dim(core_up, plane * plane_rows, plane_rows, 1)]
            + [
                lax.dynamic_slice_in_dim(core_up, (copy * depth + plane) * per_copy, per_copy, 1)
                for copy in range(copies)
            ],
            axis=1,
        )

    along = [plane_features(z)]
    for shift in range(1, depth):
        along.append(send_ring(plane_features(lax.rem(z + shift, depth)), "z", depth, shift))
    along = jnp.stack(along)

    def weight_parts(places, h, codes, *slots):
        indices = [quarter(dx, dy) * halves + h for dx, dy in places]
        return dequantize_pieces(codes, scales, indices, piece, *slots)

    given = [[weight_parts([(0, dy)], h, weight_codes) for dy in range(1, pairs)] for h in range(halves)]
    own = [weight_parts([(dx, 0) for dx in range(copies)], h, after(weight_codes, given[0][0]), pairs, y) for h in range(halves)]
    early = send_lines(*(after(groups[0], along),) * 2, range(depth - 1))
    groups = [groups[0]] + after(groups[1:], *own, *given[1])
    steps = [(jnp.concatenate(groups, axis=0),) * 2]

    up_own = along[:, :, :plane_rows]
    rows = []
    for h in range(halves):
        rows_h = [own[h]]
        for dy in range(1, pairs):
            ready = after(given[h][dy - 1], *([around[1]] if h else []))
            ready = send_ring(ready, "y", pairs, dy)
            if h == 0:
                ready = after(ready, steps[0][0])
                up_own = after(up_own, ready)
                around = [send_ring(up_own, "y", pairs, shift) for shift in range(pairs)]
            passed = [ready] + [send_ring(ready, "replica", copies, -dx) for dx in range(1, copies)]
            rows_h.append(passed)
        rows.append(rows_h)

    late = [send_lines(group, group, range(depth - 1)) for group in after(groups[1:], *early)]
    steps.append(tuple(jnp.concatenate([early[side]] + [v[side] for v in late], axis=0) for side in range(2)))
    for step in range(2, depth):
        steps.append(send_lines(*steps[-1], range(step - 1, depth - 1)))

    around = jnp.stack(around, axis=1)
    whole = jnp.zeros((depth, pairs, cores, core_rows, plane_rows), jnp.bfloat16)
    for shift in range(cores):
        whole = lax.dynamic_update_slice_in_dim(
            whole,
            send_ring(around, "local", cores, shift)[:, :, None],
            lax.rem(core - shift + cores, cores),
            2,
        )
    up_weight = whole.reshape(depth * group_rows, plane_rows)

    weight, partial = [], []
    for h in range(halves):
        half = rows[h][0]
        for dy in range(1, pairs):
            row = lax.rem(y - dy + pairs, pairs) * node_rows
            for dx, part in enumerate(rows[h][dy]):
                half = lax.dynamic_update_slice(half, part, (row, dx * piece))
        weight.append(half)
        product = contract(up_weight if h else after(up_weight, *steps[1]), weight[h], 1, 0).astype(LINK)
        partial.append(product.reshape(depth, group_rows, chain_units))

    up_sums = after(along[:, :, plane_rows:], *rows[0][1])
    up_sums = jnp.stack([send_ring(up_sums, "replica", copies, dx) for dx in range(copies)], axis=1)
    up_sums = jnp.stack([send_ring(up_sums, "y", pairs, dy) for dy in range(pairs)], axis=2)


    arrived = [steps[0][0]]
    for j in range(1, depth):
        distance, below = arrival(j)
        value = None
        for d in range((j + 1) // 2, j + 1):
            came = after(steps[d], arrived[j - 1])
            pick = jnp.where(below, came[0], came[1])
            value = pick if value is None else jnp.where(distance == d, pick, value)
        arrived.append(value)

    crossed = []
    for j in range(depth):
        ready = after(arrived[j], *(crossed[-1] if j else rows[1][1]), partial[0])
        ready = [of_quarter(ready, dx) for dx in range(copies)]
        crossed.append([send_ring(part, "replica", copies, dx) for dx, part in enumerate(ready)])
    hidden_quarter = jnp.concatenate([part for parts in crossed for part in parts], axis=0)

    up_sums = after(up_sums, *steps[depth - 1])
    whole = jnp.zeros((depth, copies, pairs, cores, core_rows, plane_rows), jnp.bfloat16)
    for shift in range(cores):
        whole = lax.dynamic_update_slice_in_dim(
            whole,
            send_ring(up_sums, "local", cores, shift)[:, :, :, None],
            lax.rem(core - shift + cores, cores),
            3,
        )
    up_sums = jnp.concatenate(
        [
            lax.dynamic_index_in_dim(whole, lax.rem(z - arrival_plane(j) + depth, depth), 0, keepdims=False)
            for j in range(depth)
        ]
    ).reshape(-1, plane_rows)

    def own_partial(goal):
        index = lax.rem(z - goal + depth, depth)
        return [lax.dynamic_index_in_dim(part, index, 0, keepdims=False) for part in partial]

    goals = [(jnp.clip(depth - step + z, 0, depth - 1), jnp.clip(step + z - depth, 0, depth - 1)) for step in range(depth)]
    first = own_partial(jnp.where(2 * z < depth, *goals[1]))
    first = [send_lines(value, value, range(1)) for value in first]
    sums = [jnp.concatenate([v[side] for v in first], axis=1) for side in range(2)]
    for step in range(2, depth):
        if step == depth - 2:
            sums = after(sums, *steps[depth - 2])
        going = [jnp.concatenate(own_partial(goals[step][side]), axis=1) + sums[side] for side in range(2)]
        if step < depth - 1:
            sums = send_lines(*going, range(step))

    out = project(after(jnp.concatenate(arrived, axis=0), *crossed[1], *crossed[2], *ready), weight)
    out = out.reshape(depth, pairs, cores, core_rows, plane_rows)
    total = lax.dynamic_index_in_dim(out, core, 2, keepdims=False).astype(jnp.float32)
    for shift in range(1, cores):
        target = lax.rem(core + shift, cores)
        total += send_ring(
            lax.dynamic_index_in_dim(out, target, 2, keepdims=False), "local", cores, shift
        ).astype(jnp.float32)
    total = total.astype(LINK)
    mine = sum(send_ring(total[:, g], "y", pairs, -g).astype(jnp.float32) for g in range(pairs)).astype(LINK)

    grads = (contract(up_sums, after(hidden_quarter), 0, 0) / float(copies)).astype(jnp.bfloat16)

    sums = []
    for h in range(halves):
        part = [value[:, h * chain_units : (h + 1) * chain_units] for value in going]
        sums.append(send_lines(*after(part, *(sums[0] if h else (out, grads))), range(depth - 1)))

    grads = grads.reshape(copies * pairs, owned_rows, part_units)
    weight_grad = jnp.zeros((owned_rows, unit_count), jnp.bfloat16)
    owned = []
    for dx in range(copies):
        for dy in range(pairs):
            chip = lax.rem(x + dx, copies) * pairs + lax.rem(y + dy, pairs)
            part = send_plane(lax.dynamic_index_in_dim(grads, chip, 0, keepdims=False), dx, dy)
            owned.append(part)
            weight_grad = lax.dynamic_update_slice_in_dim(
                weight_grad, part, quarter(-dx, -dy) * part_units, 1
            )

    own_sums = own_partial(z)
    returned = []
    for h in range(halves):
        total = sum(v.astype(jnp.float32) for v in (*after(sums[h], *owned[1 + 2 * h : 3 + h]), own_sums[h]))
        back = total.astype(LINK).reshape(pairs, tok_rows, chain_units)
        returned.append([send_ring(back[g], "y", pairs, -g) for g in range(pairs)])

    mine = after(mine, *sums[1])
    layer_out = jnp.zeros((core_rows, feature_count), jnp.bfloat16)
    for k in range(depth):
        plane = lax.rem(z - k + depth, depth)
        part = lax.dynamic_index_in_dim(mine, arrival_index(plane), 0, keepdims=False)
        part = send_ring(part, "z", depth, -k)
        layer_out = lax.dynamic_update_slice_in_dim(
            layer_out, part, lax.rem(z + k, depth) * plane_rows, 1
        )

    gate_grad = jnp.zeros((tok_rows, unit_count), jnp.bfloat16)
    up_grad = jnp.zeros((tok_rows, unit_count), jnp.bfloat16)
    for g in range(pairs):
        for h in range(halves):
            whole_part = returned[h][g]
            for dx in range(copies):
                index = quarter(dx, g) * halves + h
                part = whole_part[:, dx * piece : (dx + 1) * piece].astype(jnp.float32)
                gate_value = columns(gate_pre, index, piece).astype(jnp.float32)
                up_value = columns(up_pre, index, piece).astype(jnp.float32)
                gate_sig = jax.nn.sigmoid(gate_value)
                gate_part = part * up_value * gate_sig * (1.0 + gate_value * (1.0 - gate_sig))
                up_part = part * gate_value * gate_sig
                start = index * piece
                gate_grad = lax.dynamic_update_slice_in_dim(gate_grad, gate_part.astype(jnp.bfloat16), start, 1)
                up_grad = lax.dynamic_update_slice_in_dim(up_grad, up_part.astype(jnp.bfloat16), start, 1)
    return (layer_out, gate_grad, up_grad, weight_grad)


def solution(mesh):
    copies, nodes, cores = (mesh.shape[name] for name in ("replica", "node", "local"))
    pairs = 2
    inner = Mesh(
        mesh.devices.reshape(copies, nodes // pairs, pairs, cores), ("replica", "z", "y", "local")
    )
    tokens = ("replica", "z", "y")
    in_specs = (
        P(tokens, "local"),
        P(tokens, "local"),
        P(tokens, None),
        P(("z", "y"), "local"),
        P(("z", "y"), "local"),
    )
    out_specs = (
        P(("replica", "z", "y", "local"), None),
        P(tokens, "local"),
        P(tokens, "local"),
        P(tokens, "local"),
    )
    return jax.shard_map(
        per_device, mesh=inner, in_specs=in_specs, out_specs=out_specs, check_vma=False
    )
```

```python
import functools

import jax
import jax.numpy as jnp
from jax import lax
from jax.experimental import pallas as pl
from jax.experimental.pallas import tpu as pltpu
from jax.sharding import Mesh, PartitionSpec as P

LINK = jnp.bfloat16


def contract(left, right, left_dim, right_dim):
    return lax.dot_general(
        left, right, (((left_dim,), (right_dim,)), ((), ())), preferred_element_type=jnp.float32
    )


def project_body(steps, left_ref, *refs):
    *right_refs, out_ref, total_ref = refs
    step = pl.program_id(1)

    @pl.when(step == 0)
    def _():
        total_ref[...] = jnp.zeros_like(total_ref)

    for h, right_ref in enumerate(right_refs):

        @pl.when(lax.div(step, steps) == h)
        def _(right_ref=right_ref):
            total_ref[...] += contract(left_ref[...], right_ref[...], 1, 1)

    @pl.when(step == pl.num_programs(1) - 1)
    def _():
        out_ref[...] = total_ref[...].astype(out_ref.dtype)


def project(left, rights):
    rows = left.shape[0]
    columns, width = rights[0].shape
    row_tile, tile = 512, width // 2
    if tile % 128 or rows % row_tile or columns % 128:
        return contract(left, jnp.concatenate(rights, axis=1), 1, 1).astype(LINK)
    steps = width // tile
    flops = 2 * rows * columns * width * len(rights)
    return pl.pallas_call(
        functools.partial(project_body, steps),
        out_shape=jax.ShapeDtypeStruct((rows, columns), LINK),
        grid=(rows // row_tile, steps * len(rights)),
        in_specs=[pl.BlockSpec((row_tile, tile), lambda i, k: (i, k))]
        + [
            pl.BlockSpec((columns, tile), lambda i, k, h=h: (0, jnp.clip(k - h * steps, 0, steps - 1)))
            for h in range(len(rights))
        ],
        out_specs=pl.BlockSpec((row_tile, columns), lambda i, k: (i, 0)),
        scratch_shapes=[pltpu.VMEM((row_tile, columns), jnp.float32)],
        cost_estimate=pl.CostEstimate(flops=flops, bytes_accessed=flops // 256, transcendentals=0),
        compiler_params=pltpu.CompilerParams(vmem_limit_bytes=24 * 1024 * 1024),
    )(left, *rights)


def after(value, *others):
    return lax.optimization_barrier((value, *others))[0]


def scale_body(block, index_ref, codes_ref, scales_ref, out_ref):
    shape = (scales_ref.shape[1], codes_ref.shape[1])
    unit = lax.broadcasted_iota(jnp.int32, shape, 1) + index_ref[pl.program_id(0)] * shape[1]
    first = lax.broadcasted_iota(jnp.int32, shape, 0) * block
    owned = jnp.where((unit >= first) & (unit < first + block), 1.0, 0.0).astype(jnp.bfloat16)
    spread = jnp.dot(scales_ref[...], owned, preferred_element_type=jnp.float32)
    out_ref[...] = (codes_ref[...].astype(jnp.float32) * spread).astype(jnp.bfloat16)


def dequantize_pieces(codes, scales, indices, piece, slots=1, slot=0):
    rows = codes.shape[0]
    block = codes.shape[1] // scales.shape[1]
    if piece % 128 or rows % 256:
        whole = codes.astype(jnp.float32) * jnp.repeat(scales.astype(jnp.float32), block, axis=1)
        parts = [lax.dynamic_slice_in_dim(whole, i * piece, piece, 1) for i in indices]
        parts = jnp.concatenate(parts, axis=1).astype(jnp.bfloat16)
        return lax.dynamic_update_slice_in_dim(
            jnp.zeros((slots * rows, parts.shape[1]), jnp.bfloat16), parts, slot * rows, 0
        )
    count, tile = len(indices), 512 if rows % 512 == 0 else 256
    return pl.pallas_call(
        functools.partial(scale_body, block),
        out_shape=jax.ShapeDtypeStruct((slots * rows, count * piece), jnp.bfloat16),
        grid_spec=pltpu.PrefetchScalarGridSpec(
            num_scalar_prefetch=1,
            grid=(count, rows // tile),
            in_specs=[
                pl.BlockSpec((tile, piece), lambda i, r, index: (r, index[i])),
                pl.BlockSpec((tile, scales.shape[1]), lambda i, r, index: (r, 0)),
            ],
            out_specs=pl.BlockSpec(
                (tile, piece), lambda i, r, index: (index[count] * (rows // tile) + r, i)
            ),
        ),
        cost_estimate=pl.CostEstimate(
            flops=rows * count * piece, bytes_accessed=4 * rows * count * piece, transcendentals=0
        ),
    )(jnp.stack([*indices, jnp.asarray(slot)]).astype(jnp.int32), codes, scales)


def per_device(gate_pre, up_pre, upstream, weight_codes, scales):
    copies, depth, pairs, cores = (lax.axis_size(name) for name in ("replica", "z", "y", "local"))
    x, z, y, core = (lax.axis_index(name) for name in ("replica", "z", "y", "local"))
    above = depth - 1 - z
    tok_rows, feature_count = upstream.shape
    node_rows, unit_count = weight_codes.shape
    halves = 2
    piece = unit_count // (copies * pairs * halves)
    part_units = piece * halves
    chain_units = piece * copies
    plane_rows = node_rows * pairs
    owned_rows = feature_count // (copies * depth * pairs)
    core_rows = tok_rows // cores
    block = unit_count // scales.shape[1]
    group_rows = pairs * tok_rows

    def send_ring(value, axis, size, shift):
        if shift % size == 0:
            return value
        return lax.ppermute(value, axis, [(i, (i + shift) % size) for i in range(size)])

    def send_plane(value, dx, dy):
        moves = [
            (a * pairs + b, ((a + dx) % copies) * pairs + (b + dy) % pairs)
            for a in range(copies)
            for b in range(pairs)
        ]
        return lax.ppermute(value, ("replica", "y"), moves) if (dx, dy) != (0, 0) else value

    def send_lines(up_value, down_value, sources):
        last = depth - 1
        ups = [(i, i + 1) for i in sources]
        downs = [(last - i, last - i - 1) for i in sources]
        ends = {j for _, j in ups}
        apart = not ({i for i, _ in ups} & {i for i, _ in downs}) and not (ends & {j for _, j in downs})
        if not apart:
            return lax.ppermute(up_value, "z", ups), lax.ppermute(down_value, "z", downs)
        first = min(ends)
        if first < depth - first - 1:
            is_up, to_up = z <= max(i for i, _ in ups), z <= max(ends)
        else:
            is_up, to_up = z >= min(i for i, _ in ups), z >= first
        moved = lax.ppermute(jnp.where(is_up, up_value, down_value), "z", ups + downs)
        none = jnp.zeros_like(moved)
        return jnp.where(to_up, moved, none), jnp.where(to_up, none, moved)

    def quarter(dx, dy):
        return lax.rem(y + dy + pairs, pairs) * copies + lax.rem(x + dx + copies, copies)

    def columns(value, index, width):
        return lax.dynamic_slice_in_dim(value, index * width, width, 1)

    def of_quarter(value, dx):
        return jnp.concatenate(
            [value[:, (h * copies + dx) * piece : (h * copies + dx + 1) * piece] for h in range(halves)], axis=1
        )

    near = jnp.minimum(z, above)

    def arrival(j):
        both = j <= 2 * near
        distance = jnp.where(both, (j + 1) // 2, j - near)
        below = jnp.where(both, j % 2 == 1, z > above)
        return distance, below

    def arrival_plane(j):
        distance, below = arrival(j)
        return jnp.where(below, z - distance, z + distance)

    def arrival_index(plane):
        distance = jnp.abs(plane - z)
        return jnp.where(
            distance <= near, 2 * distance - (plane < z).astype(jnp.int32), near + distance
        )

    def hidden_part(dy):
        parts = []
        for h in range(halves):
            for dx in range(copies):
                index = quarter(dx, dy) * halves + h
                gate_value = columns(gate_pre, index, piece).astype(jnp.float32)
                up_value = columns(up_pre, index, piece).astype(jnp.float32)
                parts.append((gate_value * jax.nn.sigmoid(gate_value) * up_value).astype(jnp.bfloat16))
        return jnp.concatenate(parts, axis=1)

    hidden_parts = [hidden_part(dy) for dy in range(pairs)]
    groups = [send_ring(part, "y", pairs, dy) for dy, part in enumerate(hidden_parts)]

    core_up = lax.dynamic_slice_in_dim(after(upstream, *hidden_parts[1:]), core * core_rows, core_rows, 0)

    def plane_features(plane):
        per_copy = pairs * owned_rows
        return jnp.concatenate(
            [lax.dynamic_slice_in_dim(core_up, plane * plane_rows, plane_rows, 1)]
            + [
                lax.dynamic_slice_in_dim(core_up, (copy * depth + plane) * per_copy, per_copy, 1)
                for copy in range(copies)
            ],
            axis=1,
        )

    along = [plane_features(z)]
    for shift in range(1, depth):
        along.append(send_ring(plane_features(lax.rem(z + shift, depth)), "z", depth, shift))
    nearby = along[1]
    along = jnp.stack(along)

    def weight_parts(places, h, codes, *slots):
        indices = [quarter(dx, dy) * halves + h for dx, dy in places]
        return dequantize_pieces(codes, scales, indices, piece, *slots)

    given = [[weight_parts([(0, dy)], h, weight_codes) for dy in range(1, pairs)] for h in range(halves)]
    own = [weight_parts([(dx, 0) for dx in range(copies)], h, after(weight_codes, given[0][0], nearby), pairs, y) for h in range(halves)]
    early = send_lines(*(after(groups[0], nearby),) * 2, range(depth - 1))
    groups = [groups[0]] + after(groups[1:], *own, *given[1])
    steps = [(jnp.concatenate(groups, axis=0),) * 2]

    up_own = along[:, :, :plane_rows]
    rows = []
    for h in range(halves):
        rows_h = [own[h]]
        for dy in range(1, pairs):
            ready = after(given[h][dy - 1], *([around[1]] if h else []))
            ready = send_ring(ready, "y", pairs, dy)
            if h == 0:
                ready = after(ready, steps[0][0])
                up_own = after(up_own, ready)
                around = [send_ring(up_own, "y", pairs, shift) for shift in range(pairs)]
            passed = [ready] + [send_ring(ready, "replica", copies, -dx) for dx in range(1, copies)]
            rows_h.append(passed)
        rows.append(rows_h)

    late = [send_lines(group, group, range(depth - 1)) for group in after(groups[1:], *early)]
    steps.append(tuple(jnp.concatenate([early[side]] + [v[side] for v in late], axis=0) for side in range(2)))
    for step in range(2, depth):
        steps.append(send_lines(*steps[-1], range(step - 1, depth - 1)))

    around = jnp.stack(around, axis=1)
    whole = jnp.zeros((depth, pairs, cores, core_rows, plane_rows), jnp.bfloat16)
    for shift in range(cores):
        whole = lax.dynamic_update_slice_in_dim(
            whole,
            send_ring(around, "local", cores, shift)[:, :, None],
            lax.rem(core - shift + cores, cores),
            2,
        )
    up_weight = whole.reshape(depth * group_rows, plane_rows)

    weight, partial = [], []
    for h in range(halves):
        half = rows[h][0]
        for dy in range(1, pairs):
            row = lax.rem(y - dy + pairs, pairs) * node_rows
            for dx, part in enumerate(rows[h][dy]):
                half = lax.dynamic_update_slice(half, part, (row, dx * piece))
        weight.append(half)
        product = contract(up_weight if h else after(up_weight, *steps[1]), weight[h], 1, 0).astype(LINK)
        partial.append(product.reshape(depth, group_rows, chain_units))

    up_sums = after(along[:, :, plane_rows:], *rows[0][1])
    up_sums = jnp.stack([send_ring(up_sums, "replica", copies, dx) for dx in range(copies)], axis=1)
    up_sums = jnp.stack([send_ring(up_sums, "y", pairs, dy) for dy in range(pairs)], axis=2)


    arrived = [steps[0][0]]
    for j in range(1, depth):
        distance, below = arrival(j)
        value = None
        for d in range((j + 1) // 2, j + 1):
            came = after(steps[d], arrived[j - 1])
            pick = jnp.where(below, came[0], came[1])
            value = pick if value is None else jnp.where(distance == d, pick, value)
        arrived.append(value)

    crossed = []
    for j in range(depth):
        ready = after(arrived[j], *(crossed[-1] if j else rows[1][1]), partial[0])
        ready = [of_quarter(ready, dx) for dx in range(copies)]
        crossed.append([send_ring(part, "replica", copies, dx) for dx, part in enumerate(ready)])
    hidden_quarter = jnp.concatenate([part for parts in crossed for part in parts], axis=0)

    up_sums = after(up_sums, *steps[depth - 1])
    whole = jnp.zeros((depth, copies, pairs, cores, core_rows, plane_rows), jnp.bfloat16)
    for shift in range(cores):
        whole = lax.dynamic_update_slice_in_dim(
            whole,
            send_ring(up_sums, "local", cores, shift)[:, :, :, None],
            lax.rem(core - shift + cores, cores),
            3,
        )
    up_sums = jnp.concatenate(
        [
            lax.dynamic_index_in_dim(whole, lax.rem(z - arrival_plane(j) + depth, depth), 0, keepdims=False)
            for j in range(depth)
        ]
    ).reshape(-1, plane_rows)

    def own_partial(goal):
        index = lax.rem(z - goal + depth, depth)
        return [lax.dynamic_index_in_dim(part, index, 0, keepdims=False) for part in partial]

    goals = [(jnp.clip(depth - step + z, 0, depth - 1), jnp.clip(step + z - depth, 0, depth - 1)) for step in range(depth)]
    first = own_partial(jnp.where(2 * z < depth, *goals[1]))
    first = [send_lines(value, value, range(1)) for value in first]
    sums = [jnp.concatenate([v[side] for v in first], axis=1) for side in range(2)]
    for step in range(2, depth):
        if step == depth - 2:
            sums = after(sums, *steps[depth - 2])
        going = [jnp.concatenate(own_partial(goals[step][side]), axis=1) + sums[side] for side in range(2)]
        if step < depth - 1:
            sums = send_lines(*going, range(step))

    out = project(after(jnp.concatenate(arrived, axis=0), *crossed[1], *crossed[2], *ready), weight)
    out = out.reshape(depth, pairs, cores, core_rows, plane_rows)
    total = lax.dynamic_index_in_dim(out, core, 2, keepdims=False).astype(jnp.float32)
    for shift in range(1, cores):
        target = lax.rem(core + shift, cores)
        total += send_ring(
            lax.dynamic_index_in_dim(out, target, 2, keepdims=False), "local", cores, shift
        ).astype(jnp.float32)
    total = total.astype(LINK)
    mine = sum(send_ring(total[:, g], "y", pairs, -g).astype(jnp.float32) for g in range(pairs)).astype(LINK)

    grads = (contract(up_sums, after(hidden_quarter), 0, 0) / float(copies)).astype(jnp.bfloat16)

    sums = []
    for h in range(halves):
        part = [value[:, h * chain_units : (h + 1) * chain_units] for value in going]
        sums.append(send_lines(*after(part, *(sums[0] if h else (out, grads))), range(depth - 1)))

    grads = grads.reshape(copies * pairs, owned_rows, part_units)
    weight_grad = jnp.zeros((owned_rows, unit_count), jnp.bfloat16)
    owned = []
    for dx in range(copies):
        for dy in range(pairs):
            chip = lax.rem(x + dx, copies) * pairs + lax.rem(y + dy, pairs)
            part = send_plane(lax.dynamic_index_in_dim(grads, chip, 0, keepdims=False), dx, dy)
            owned.append(part)
            weight_grad = lax.dynamic_update_slice_in_dim(
                weight_grad, part, quarter(-dx, -dy) * part_units, 1
            )

    own_sums = own_partial(z)
    returned = []
    for h in range(halves):
        total = sum(v.astype(jnp.float32) for v in (*after(sums[h], *owned[1 + 2 * h : 3 + h]), own_sums[h]))
        back = total.astype(LINK).reshape(pairs, tok_rows, chain_units)
        returned.append([send_ring(back[g], "y", pairs, -g) for g in range(pairs)])

    mine = after(mine, *sums[1])
    layer_out = jnp.zeros((core_rows, feature_count), jnp.bfloat16)
    for k in range(depth):
        plane = lax.rem(z - k + depth, depth)
        part = lax.dynamic_index_in_dim(mine, arrival_index(plane), 0, keepdims=False)
        part = send_ring(part, "z", depth, -k)
        layer_out = lax.dynamic_update_slice_in_dim(
            layer_out, part, lax.rem(z + k, depth) * plane_rows, 1
        )

    gate_grad = jnp.zeros((tok_rows, unit_count), jnp.bfloat16)
    up_grad = jnp.zeros((tok_rows, unit_count), jnp.bfloat16)
    for g in range(pairs):
        for h in range(halves):
            whole_part = returned[h][g]
            for dx in range(copies):
                index = quarter(dx, g) * halves + h
                part = whole_part[:, dx * piece : (dx + 1) * piece].astype(jnp.float32)
                gate_value = columns(gate_pre, index, piece).astype(jnp.float32)
                up_value = columns(up_pre, index, piece).astype(jnp.float32)
                gate_sig = jax.nn.sigmoid(gate_value)
                gate_part = part * up_value * gate_sig * (1.0 + gate_value * (1.0 - gate_sig))
                up_part = part * gate_value * gate_sig
                start = index * piece
                gate_grad = lax.dynamic_update_slice_in_dim(gate_grad, gate_part.astype(jnp.bfloat16), start, 1)
                up_grad = lax.dynamic_update_slice_in_dim(up_grad, up_part.astype(jnp.bfloat16), start, 1)
    return (layer_out, gate_grad, up_grad, weight_grad)


def solution(mesh):
    copies, nodes, cores = (mesh.shape[name] for name in ("replica", "node", "local"))
    pairs = 2
    inner = Mesh(
        mesh.devices.reshape(copies, nodes // pairs, pairs, cores), ("replica", "z", "y", "local")
    )
    tokens = ("replica", "z", "y")
    in_specs = (
        P(tokens, "local"),
        P(tokens, "local"),
        P(tokens, None),
        P(("z", "y"), "local"),
        P(("z", "y"), "local"),
    )
    out_specs = (
        P(("replica", "z", "y", "local"), None),
        P(tokens, "local"),
        P(tokens, "local"),
        P(tokens, "local"),
    )
    return jax.shard_map(
        per_device, mesh=inner, in_specs=in_specs, out_specs=out_specs, check_vma=False
    )
```
